32 devices in a mesh: blk: 4 (over z), section: 8 (over y, x, core).
Axes of the slice: x: 2, y: 2, z: 4, core: 2. Of those that a mesh axis runs over, the one named last changes fastest.
Arguments:
- text_emb: bfloat16 [8, 1024, 1024], P(None, ('blk', 'section')), may hold values from -6 to 6
- covariate: bfloat16 [8, 256, 1024], P('section', 'blk'), may hold values from -6 to 6
- labels: int32 [8, 1024], P('section', 'blk'), may hold values from 0 to 255, as said below
- logit_scale: float32 [1], replicated, may hold values from 0.02 to 0.08
- logit_bias: float32 [1], replicated, may hold values from -3 to -1
Outputs:
- text_grad: float32 [8, 1024, 1024], P('section', 'blk')
- cov_grad: float32 [8, 256, 1024], P('section', 'blk')
The draws below stay inside these ranges and needn't reach their ends.
Inputs may be any that keep to these rules, and one draw needn't show every extreme that they name: `labels`: every covariate row of a group is the positive of exactly 4 text rows of that group.
All inputs are finite; a program needn't handle non-finite values.
Results may differ from the reference program's by a relative error of at most 0.0025.
Values may be sent and summed in bfloat16 or wider, within the bound.
No kernel may reach another device: no remote copies, remote signals or barrier semaphores. Data moves between devices by JAX's collectives and lax.ppermute only.
A program may use at most 64 MiB of HBM per device.

```python
import math
import jax
import jax.numpy as jnp
from jax import lax

D = 1024
COV_DEV = 64
TXT_GROUP = 1024
COV_GROUP = 256
N_BLK = 4
N_SECTION = 8


def draw_labels(key, part):
    group_keys = jax.random.split(key, N_SECTION)
    orders = jax.vmap(lambda one_key: jax.random.permutation(one_key, TXT_GROUP))(group_keys)
    return (orders.astype(jnp.int32) % COV_GROUP).astype(jnp.int32)


def shard_levels(own_key, dims, cuts, least, high):
    level, own = 1.0, jax.random.fold_in(own_key, 6)
    for axis_at, parts in cuts:
        draws = jnp.exp(jax.random.uniform(jax.random.fold_in(own, axis_at), (parts,), jnp.float32, least / len(cuts), high / len(cuts)))
        level = level * jnp.repeat(draws, dims[axis_at] // parts).reshape([-1 if axis == axis_at else 1 for axis in range(len(dims))])
    return level


def noise(rng, shape, scale, limit, shards=(), kind=jnp.bfloat16):
    gain = shard_levels(rng, shape, shards, -0.22, 0.18) if shards else 1.0
    result = jax.random.normal(rng, shape, jnp.float32) * scale * gain
    return jnp.minimum(jnp.maximum(result, -limit), limit).astype(kind)


def setup_inputs(seed: int = 0) -> dict:
    key_of = jax.random.split(jax.random.key(seed), 6)
    return {
        "text_emb": noise(key_of[0], (N_SECTION, TXT_GROUP, D), 1.0, 6.0, ((1, 32),)),
        "covariate": noise(key_of[1], (N_SECTION, COV_GROUP, D), 1.0, 6.0, ((0, 8), (1, 4))),
        "labels": draw_labels(jax.random.fold_in(key_of[5], 71), 0),
        "logit_scale": jnp.clip(jnp.exp(jax.random.uniform(key_of[3], (1,), jnp.float32, math.log(0.02), math.log(0.08))), 0.02, 0.08),
        "logit_bias": jnp.clip(jax.random.uniform(key_of[4], (1,), jnp.float32, -3.0, -1.0), -3.0, -1.0),
    }


def reference(text_emb, covariate, labels, logit_scale, logit_bias):
    factor = logit_scale[0]
    offset = logit_bias[0]
    block_ids = jnp.arange(COV_GROUP, dtype=jnp.int32).reshape(N_BLK, COV_DEV)

    def one_group(group_in):
        text_rows, cov_rows, group_labels = group_in
        cov_blocks = cov_rows.reshape(N_BLK, COV_DEV, D)

        def block_step(text_acc, blocks_in):
            cov_block, row_ids = blocks_in
            logits = factor * jnp.dot(cov_block, text_rows.T, preferred_element_type=jnp.float32) + offset
            positive = (group_labels[None, :] == row_ids[:, None]).astype(jnp.float32)
            weights_bf = (factor * (jax.nn.sigmoid(logits) - positive)).astype(jnp.bfloat16)
            cov_term = jnp.dot(weights_bf, text_rows, preferred_element_type=jnp.float32)
            text_acc = text_acc + jnp.dot(weights_bf.T, cov_block, preferred_element_type=jnp.float32)
            return text_acc, cov_term

        start_acc = jnp.zeros((TXT_GROUP, D), jnp.float32)
        text_part, cov_terms = lax.scan(block_step, start_acc, (cov_blocks, block_ids))
        return text_part, cov_terms.reshape(COV_GROUP, D)

    text_grad, cov_grad = lax.map(one_group, (text_emb, covariate, labels))
    return text_grad, cov_grad
```

```python
import functools
import jax
import jax.numpy as jnp
from jax import lax
from jax.experimental import pallas as pl
from jax.experimental.pallas import tpu as pltpu
from jax.sharding import PartitionSpec as P

NT = (((1,), (1,)), ((), ()))
TN = (((0,), (0,)), ((), ()))


def hops(count):
    if count & (count - 1) == 0:
        return [[(i, i ^ k) for i in range(count)] for k in range(1, count)]
    return [[(i, (i + k) % count) for i in range(count)] for k in range(1, count)]


def block_of(me, k, count):
    return me ^ k if count & (count - 1) == 0 else (me - k + count) % count


def block_to(me, k, count):
    return me ^ k if count & (count - 1) == 0 else (me + k) % count


def coeff_kernel(count, rows, scale_ref, bias_ref, labels_ref, panel_ref, *refs):
    covs, (coeff_ref, own_ref), parts = refs[:count], refs[count:count + 2], refs[count + 2:]
    me = lax.axis_index("blk")
    scale, bias = scale_ref[0], bias_ref[0]
    panel = panel_ref[...]
    labels = labels_ref[...]
    for k in range(count):
        logits = scale * lax.dot_general(covs[k][...], panel, NT, preferred_element_type=jnp.float32) + bias
        ids = block_of(me, k, count) * rows + lax.broadcasted_iota(jnp.int32, logits.shape, 0)
        positive = (labels == ids).astype(jnp.float32)
        coeff = (scale * (jax.nn.sigmoid(logits) - positive)).astype(jnp.bfloat16)
        coeff_ref[k * rows:(k + 1) * rows, :] = coeff
        term = jnp.dot(coeff, panel, preferred_element_type=jnp.float32)
        if k == 0:
            own_ref[...] = term
        else:
            parts[k - 1][...] = term.astype(jnp.bfloat16)


def text_kernel(count, rows, coeff_ref, *refs):
    covs, out_ref = refs[:count], refs[count]
    total = None
    for k in range(count):
        term = lax.dot_general(coeff_ref[k * rows:(k + 1) * rows, :], covs[k][...], TN, preferred_element_type=jnp.float32)
        total = term if total is None else total + term
    out_ref[...] = total


def local(text_emb, covariate, labels, logit_scale, logit_bias):
    count = lax.axis_size("blk")
    rows, width = covariate.shape[1:]
    covs = [covariate[0]] + [lax.ppermute(covariate[0], "blk", p) for p in hops(count)]
    panel = lax.all_to_all(text_emb, "section", 0, 0, tiled=True).reshape(-1, width)
    texts = panel.shape[0]
    vmem = pl.BlockSpec(memory_space=pltpu.VMEM)
    smem = pl.BlockSpec(memory_space=pltpu.SMEM)
    coeff, own, *parts = pl.pallas_call(
        functools.partial(coeff_kernel, count, rows),
        out_shape=[jax.ShapeDtypeStruct((count * rows, texts), jnp.bfloat16), jax.ShapeDtypeStruct((rows, width), jnp.float32)]
        + [jax.ShapeDtypeStruct((rows, width), jnp.bfloat16)] * (count - 1),
        in_specs=[smem, smem] + [vmem] * (2 + count),
        out_specs=[vmem] * (1 + count),
        compiler_params=pltpu.CompilerParams(vmem_limit_bytes=32 * 2**20),
        cost_estimate=pl.CostEstimate(flops=4 * count * rows * texts * width, bytes_accessed=2**20, transcendentals=0),
        name="coeff",
    )(logit_scale, logit_bias, labels, panel, *covs)
    got = [lax.ppermute(part, "blk", p) for part, p in zip(parts, hops(count))]
    text_grad = pl.pallas_call(
        functools.partial(text_kernel, count, rows),
        out_shape=jax.ShapeDtypeStruct((texts, width), jnp.float32),
        in_specs=[vmem] * (1 + count),
        out_specs=vmem,
        compiler_params=pltpu.CompilerParams(vmem_limit_bytes=32 * 2**20),
        cost_estimate=pl.CostEstimate(flops=2 * count * rows * texts * width, bytes_accessed=2**20, transcendentals=0),
        name="text_grad",
    )(coeff, *covs)
    total = own
    for part in got:
        total = total + part.astype(jnp.float32)
    return text_grad[None], total[None]


def solution(mesh):
    return jax.shard_map(
        local,
        mesh=mesh,
        in_specs=(
            P(None, ("blk", "section"), None),
            P("section", "blk", None),
            P("section", "blk"),
            P(),
            P(),
        ),
        out_specs=(P("section", "blk", None), P("section", "blk", None)),
        check_vma=False,
    )
```

```python
import functools

import jax
import jax.numpy as jnp
from jax import lax
from jax.experimental import pallas as pl
from jax.experimental.pallas import tpu as pltpu
from jax.sharding import PartitionSpec as P

NT = (((1,), (1,)), ((), ()))
TN = (((0,), (0,)), ((), ()))
VMEM = pl.BlockSpec(memory_space=pltpu.VMEM)
ANY = pl.BlockSpec(memory_space=pl.ANY)
MIB = 2**20
BF16, F32 = jnp.bfloat16, jnp.float32
SHAPE = jax.ShapeDtypeStruct
LONG = 10**11


def is_power(count):
    return count & (count - 1) == 0


def exchange(value, axis, k):
    count = lax.axis_size(axis)
    return lax.ppermute(value, axis, [(i, i ^ k if is_power(count) else (i + k) % count) for i in range(count)])


def source_block(me, k, count):
    return me ^ k if is_power(count) else lax.rem(me - k + count, jnp.int32(count))


def span(slot, rows):
    return pl.ds(pl.multiple_of(slot * rows, rows), rows)


def select_kernel(chips, *refs):
    core = lax.axis_index("section") % 2
    out = refs[-1]
    for k in range(chips):
        out[k] = refs[k][1 - core]


def pile_kernel(*refs):
    *parts, out = refs
    rows = parts[0].shape[0]
    for k, part in enumerate(parts):
        out[k * rows:(k + 1) * rows, :] = part[...]


def coeff_kernel(count, chips, params_ref, covs_ref, *refs):
    texts, (coeff_ref, own_ref, *part_refs, panel, prod) = refs[:chips + 1], refs[chips + 1:]
    rows = covs_ref.shape[0] // count
    if chips:
        section = lax.axis_index("section")
        chip, core = section // 2, section % 2
        piece = texts[0].shape[1]
        for k in range(chips):
            panel[span((chip ^ k) * 2 + core, piece), :] = texts[k][core]
            panel[span((chip ^ k) * 2 + 1 - core, piece), :] = texts[chips][k]
        text = panel[...]
    else:
        text = texts[0][...]
    labels, scale, bias = params_ref[0:1, :], params_ref[1:2, :], params_ref[2:3, :]
    logits = scale * lax.dot_general(covs_ref[...], text, NT, preferred_element_type=F32) + bias
    me = lax.axis_index("blk")
    row = lax.broadcasted_iota(jnp.int32, (rows, 1), 0)
    ids = jnp.concatenate([source_block(me, k, count) * rows + row for k in range(count)], axis=0)
    positive = (labels == ids.astype(F32)).astype(F32)
    coeff = (scale * (jax.nn.sigmoid(logits) - positive)).astype(BF16)
    coeff_ref[...] = coeff
    prod[...] = jnp.dot(coeff, text, preferred_element_type=F32)
    own_ref[...] = prod[0:rows, :]
    for k, ref in enumerate(part_refs, 1):
        ref[...] = prod[k * rows:(k + 1) * rows, :].astype(BF16)


def text_kernel(coeff_ref, covs_ref, out_ref):
    out_ref[...] = lax.dot_general(coeff_ref[...], covs_ref[...], TN, preferred_element_type=F32)


def call(kernel, name, out_shape, args, flops, scratch=(), limit=8, specs=None):
    many = isinstance(out_shape, list)
    return pl.pallas_call(
        kernel,
        out_shape=out_shape,
        in_specs=specs or [VMEM] * len(args),
        out_specs=[VMEM] * len(out_shape) if many else VMEM,
        scratch_shapes=list(scratch),
        compiler_params=pltpu.CompilerParams(vmem_limit_bytes=limit * MIB),
        cost_estimate=pl.CostEstimate(flops=flops, bytes_accessed=MIB, transcendentals=0),
        name=name,
    )(*args)


def fetch_covs(own, count):
    if count != 4:
        return [own] + [exchange(own, "blk", k) for k in range(1, count)], []
    far = exchange(own, "blk", 3)
    return [own, exchange(own, "blk", 1), exchange(far, "blk", 1), far], [far]


def fetch_texts(text_emb, early):
    groups, piece, width = text_emb.shape
    if not is_power(groups) or piece % 16:
        return [lax.all_to_all(text_emb, "section", 0, 0, tiled=True).reshape(-1, width)], 0
    chips = groups // 2
    chip = lax.axis_index("section") // 2
    by_chip = text_emb.reshape(chips, 2, piece, width)
    parts = [lax.dynamic_index_in_dim(by_chip, chip ^ k, 0, keepdims=False) for k in range(chips)]
    texts = parts[:1] + [exchange(parts[k], "section", 2 * k) for k in range(1, chips)]
    other = call(
        functools.partial(select_kernel, chips), "select", SHAPE((chips, piece, width), BF16),
        texts + early, LONG, specs=[VMEM] * chips + [ANY] * len(early))
    return texts + [exchange(other, "section", 1)], chips


def local(text_emb, covariate, labels, logit_scale, logit_bias):
    count = lax.axis_size("blk")
    rows, width = covariate.shape[1:]
    n_text = labels.shape[1]
    params = jnp.concatenate(
        [labels.astype(F32), jnp.broadcast_to(logit_scale[None], labels.shape), jnp.broadcast_to(logit_bias[None], labels.shape)])
    params = jnp.pad(params, ((0, 5), (0, 0)))
    covs, early = fetch_covs(covariate[0], count)
    texts, chips = fetch_texts(text_emb, early + [params])
    pile = call(pile_kernel, "pile", SHAPE((count * rows, width), BF16), covs, LONG)
    flops = 2 * count * rows * n_text * width
    coeff, own, *parts = call(
        functools.partial(coeff_kernel, count, chips), "coeff",
        [SHAPE((count * rows, n_text), BF16), SHAPE((rows, width), F32)] + [SHAPE((rows, width), BF16)] * (count - 1),
        [params, pile] + texts, 2 * flops, limit=16 if count == 4 else 40,
        scratch=[pltpu.VMEM((n_text, width) if chips else (8, 128), BF16), pltpu.VMEM((count * rows, width), F32)])
    got = [exchange(part, "blk", k if is_power(count) else -k) for k, part in enumerate(parts, 1)]
    text_grad = call(text_kernel, "text_grad", SHAPE((n_text, width), F32), [coeff, pile], flops, limit=16)
    total = own
    for part in got:
        total = total + part.astype(F32)
    return text_grad[None], total[None]


def solution(mesh):
    return jax.shard_map(
        local,
        mesh=mesh,
        in_specs=(
            P(None, ("blk", "section"), None),
            P("section", "blk", None),
            P("section", "blk"),
            P(),
            P(),
        ),
        out_specs=(P("section", "blk", None), P("section", "blk", None)),
        check_vma=False,
    )
```

```python
import functools

import jax
import jax.numpy as jnp
from jax import lax
from jax.experimental import pallas as pl
from jax.experimental.pallas import tpu as pltpu
from jax.sharding import PartitionSpec as P

NT = (((1,), (1,)), ((), ()))
TN = (((0,), (0,)), ((), ()))
VMEM = pl.BlockSpec(memory_space=pltpu.VMEM)
ANY = pl.BlockSpec(memory_space=pl.ANY)
MIB = 2**20
BF16, F32 = jnp.bfloat16, jnp.float32
SHAPE = jax.ShapeDtypeStruct
LONG = 10**11


def is_power(count):
    return count & (count - 1) == 0


def exchange(value, axis, k):
    count = lax.axis_size(axis)
    return lax.ppermute(value, axis, [(i, i ^ k if is_power(count) else (i + k) % count) for i in range(count)])


def source_block(me, k, count):
    return me ^ k if is_power(count) else lax.rem(me - k + count, jnp.int32(count))


def span(slot, rows):
    return pl.ds(pl.multiple_of(slot * rows, rows), rows)


def select_kernel(chips, *refs):
    core = lax.axis_index("section") % 2
    out = refs[-1]
    for k in range(chips):
        out[k] = refs[k][1 - core]


def pile_kernel(*refs):
    *parts, out = refs
    rows = parts[0].shape[0]
    for k, part in enumerate(parts):
        out[k * rows:(k + 1) * rows, :] = part[...]


def coeff_kernel(count, chips, params_ref, covs_ref, *refs):
    texts, (coeff_ref, own_ref, *part_refs, panel, prod) = refs[:chips + 1], refs[chips + 1:]
    rows = covs_ref.shape[0] // count
    if chips:
        section = lax.axis_index("section")
        chip, core = section // 2, section % 2
        piece = texts[0].shape[1]
        for k in range(chips):
            panel[span((chip ^ k) * 2 + core, piece), :] = texts[k][core]
            panel[span((chip ^ k) * 2 + 1 - core, piece), :] = texts[chips][k]
        text = panel[...]
    else:
        text = texts[0][...]
    labels, scale, bias = params_ref[0:1, :], params_ref[1:2, :], params_ref[2:3, :]
    logits = scale * lax.dot_general(covs_ref[...], text, NT, preferred_element_type=F32) + bias
    me = lax.axis_index("blk")
    row = lax.broadcasted_iota(jnp.int32, (rows, 1), 0)
    ids = jnp.concatenate([source_block(me, k, count) * rows + row for k in range(count)], axis=0)
    positive = (labels == ids.astype(F32)).astype(F32)
    coeff = (scale * (jax.nn.sigmoid(logits) - positive)).astype(BF16)
    coeff_ref[...] = coeff
    prod[...] = jnp.dot(coeff, text, preferred_element_type=F32)
    own_ref[...] = prod[0:rows, :]
    for k, ref in enumerate(part_refs, 1):
        ref[...] = prod[k * rows:(k + 1) * rows, :].astype(BF16)


def text_kernel(coeff_ref, covs_ref, out_ref):
    out_ref[...] = lax.dot_general(coeff_ref[...], covs_ref[...], TN, preferred_element_type=F32)


def call(kernel, name, out_shape, args, flops, scratch=(), limit=8, specs=None):
    many = isinstance(out_shape, list)
    return pl.pallas_call(
        kernel,
        out_shape=out_shape,
        in_specs=specs or [VMEM] * len(args),
        out_specs=[VMEM] * len(out_shape) if many else VMEM,
        scratch_shapes=list(scratch),
        compiler_params=pltpu.CompilerParams(vmem_limit_bytes=limit * MIB),
        cost_estimate=pl.CostEstimate(flops=flops, bytes_accessed=MIB, transcendentals=0),
        name=name,
    )(*args)


def fetch_covs(own, count):
    if count != 4:
        return [own] + [exchange(own, "blk", k) for k in range(1, count)], []
    two = exchange(own, "blk", 2)
    return [own, exchange(own, "blk", 1), two, exchange(two, "blk", 1)], [two]


def fetch_texts(text_emb, early):
    groups, piece, width = text_emb.shape
    if not is_power(groups) or piece % 16:
        return [lax.all_to_all(text_emb, "section", 0, 0, tiled=True).reshape(-1, width)], 0
    chips = groups // 2
    chip = lax.axis_index("section") // 2
    by_chip = text_emb.reshape(chips, 2, piece, width)
    parts = [lax.dynamic_index_in_dim(by_chip, chip ^ k, 0, keepdims=False) for k in range(chips)]
    texts = parts[:1] + [exchange(parts[k], "section", 2 * k) for k in range(1, chips)]
    other = call(
        functools.partial(select_kernel, chips), "select", SHAPE((chips, piece, width), BF16),
        texts + early, LONG, specs=[VMEM] * chips + [ANY] * len(early))
    return texts + [exchange(other, "section", 1)], chips


def local(text_emb, covariate, labels, logit_scale, logit_bias):
    count = lax.axis_size("blk")
    rows, width = covariate.shape[1:]
    n_text = labels.shape[1]
    params = jnp.concatenate(
        [labels.astype(F32), jnp.broadcast_to(logit_scale[None], labels.shape), jnp.broadcast_to(logit_bias[None], labels.shape)])
    params = jnp.pad(params, ((0, 5), (0, 0)))
    covs, early = fetch_covs(covariate[0], count)
    texts, chips = fetch_texts(text_emb, early + [params])
    pile = call(pile_kernel, "pile", SHAPE((count * rows, width), BF16), covs, LONG)
    flops = 2 * count * rows * n_text * width
    coeff, own, *parts = call(
        functools.partial(coeff_kernel, count, chips), "coeff",
        [SHAPE((count * rows, n_text), BF16), SHAPE((rows, width), F32)] + [SHAPE((rows, width), BF16)] * (count - 1),
        [params, pile] + texts, 2 * flops, limit=16 if count == 4 else 40,
        scratch=[pltpu.VMEM((n_text, width) if chips else (8, 128), BF16), pltpu.VMEM((count * rows, width), F32)])
    order = (2, 1, 3) if count == 4 else range(1, count)
    got = [exchange(parts[k - 1], "blk", k if is_power(count) else -k) for k in order]
    text_grad = call(text_kernel, "text_grad", SHAPE((n_text, width), F32), [coeff, pile], flops, limit=16)
    total = own
    for part in got:
        total = total + part.astype(F32)
    return text_grad[None], total[None]


def solution(mesh):
    return jax.shard_map(
        local,
        mesh=mesh,
        in_specs=(
            P(None, ("blk", "section"), None),
            P("section", "blk", None),
            P("section", "blk"),
            P(),
            P(),
        ),
        out_specs=(P("section", "blk", None), P("section", "blk", None)),
        check_vma=False,
    )
```

```python
import functools

import jax
import jax.numpy as jnp
from jax import lax
from jax.experimental import pallas as pl
from jax.experimental.pallas import tpu as pltpu
from jax.sharding import PartitionSpec as P

NT = (((1,), (1,)), ((), ()))
TN = (((0,), (0,)), ((), ()))
VMEM = pl.BlockSpec(memory_space=pltpu.VMEM)
ANY = pl.BlockSpec(memory_space=pl.ANY)
MIB = 2**20
BF16, F32 = jnp.bfloat16, jnp.float32
SHAPE = jax.ShapeDtypeStruct
LONG = 10**11


def is_power(count):
    return count & (count - 1) == 0


def exchange(value, axis, k):
    count = lax.axis_size(axis)
    return lax.ppermute(value, axis, [(i, i ^ k if is_power(count) else (i + k) % count) for i in range(count)])


def mixed(value, even, odd):
    blocks, groups = lax.axis_size("blk"), lax.axis_size("section")
    steps = [odd if s % 2 else even for s in range(groups)]
    pairs = [(b * groups + s, (b ^ steps[s]) * groups + s) for b in range(blocks) for s in range(groups) if steps[s]]
    return lax.ppermute(value, ("blk", "section"), pairs)


def source_block(me, k, count):
    return me ^ k if is_power(count) else lax.rem(me - k + count, jnp.int32(count))


def span(slot, rows):
    return pl.ds(pl.multiple_of(slot * rows, rows), rows)


def select_kernel(chips, *refs):
    core = lax.axis_index("section") % 2
    out = refs[-1]
    for k in range(chips):
        out[k] = refs[k][1 - core]


def pile_kernel(*refs):
    *parts, out = refs
    rows = parts[0].shape[0]
    for k, part in enumerate(parts):
        out[k * rows:(k + 1) * rows, :] = part[...]


def coeff_kernel(count, chips, params_ref, covs_ref, *refs):
    texts, (coeff_ref, own_ref, *part_refs, panel, prod) = refs[:chips + 1], refs[chips + 1:]
    rows = covs_ref.shape[0] // count
    if chips:
        section = lax.axis_index("section")
        chip, core = section // 2, section % 2
        piece = texts[0].shape[1]
        for k in range(chips):
            panel[span((chip ^ k) * 2 + core, piece), :] = texts[k][core]
            panel[span((chip ^ k) * 2 + 1 - core, piece), :] = texts[chips][k]
        text = panel[...]
    else:
        text = texts[0][...]
    labels, scale, bias = params_ref[0:1, :], params_ref[1:2, :], params_ref[2:3, :]
    logits = scale * lax.dot_general(covs_ref[...], text, NT, preferred_element_type=F32) + bias
    me = lax.axis_index("blk")
    row = lax.broadcasted_iota(jnp.int32, (rows, 1), 0)
    ids = jnp.concatenate([source_block(me, k, count) * rows + row for k in range(count)], axis=0)
    positive = (labels == ids.astype(F32)).astype(F32)
    coeff = (scale * (jax.nn.sigmoid(logits) - positive)).astype(BF16)
    coeff_ref[...] = coeff
    prod[...] = jnp.dot(coeff, text, preferred_element_type=F32)
    own_ref[...] = prod[0:rows, :]
    if two_cores(count):
        odd = lax.axis_index("section") % 2
        first, second, third, far = part_refs
        first[...] = prod[2 * rows:3 * rows, :].astype(BF16)
        second[...] = prod[span(3 - 2 * odd, rows), :].astype(BF16)
        third[...] = prod[rows:2 * rows, :].astype(BF16)
        far[...] = prod[3 * rows:4 * rows, :]
    else:
        for k, ref in enumerate(part_refs, 1):
            ref[...] = prod[k * rows:(k + 1) * rows, :].astype(BF16)


def add_kernel(part_ref, got_ref, out_ref):
    out_ref[...] = (part_ref[...] + got_ref[...].astype(F32)).astype(BF16)


def text_kernel(coeff_ref, covs_ref, out_ref):
    out_ref[...] = lax.dot_general(coeff_ref[...], covs_ref[...], TN, preferred_element_type=F32)


def call(kernel, name, out_shape, args, flops, scratch=(), limit=8, specs=None):
    many = isinstance(out_shape, list)
    return pl.pallas_call(
        kernel,
        out_shape=out_shape,
        in_specs=specs or [VMEM] * len(args),
        out_specs=[VMEM] * len(out_shape) if many else VMEM,
        scratch_shapes=list(scratch),
        compiler_params=pltpu.CompilerParams(vmem_limit_bytes=limit * MIB),
        cost_estimate=pl.CostEstimate(flops=flops, bytes_accessed=MIB, transcendentals=0),
        name=name,
    )(*args)


def two_cores(count):
    return count == 4 and lax.axis_size("section") % 2 == 0


def reduce_covs(own, parts, count):
    if not two_cores(count):
        got = [exchange(part, "blk", k if is_power(count) else -k) for k, part in enumerate(parts, 1)]
        return sum((part.astype(F32) for part in got), own)
    first, second, third, far = parts
    got = [mixed(first, 2, 1), mixed(second, 3, 1), mixed(third, 1, 0)]
    summed = call(add_kernel, "add", SHAPE(far.shape, BF16), [far, got[0]], 0)
    got.append(mixed(summed, 0, 3))
    odd = lax.axis_index("section") % 2 == 1
    return own + jnp.where(odd, 0, got[0].astype(F32)) + sum(part.astype(F32) for part in got[1:])


def fetch_covs(own, count):
    if count != 4:
        return [own] + [exchange(own, "blk", k) for k in range(1, count)], []
    two = exchange(own, "blk", 2)
    return [own, exchange(own, "blk", 1), two, exchange(two, "blk", 1)], [two]


def fetch_texts(text_emb, early):
    groups, piece, width = text_emb.shape
    if not is_power(groups) or piece % 16:
        return [lax.all_to_all(text_emb, "section", 0, 0, tiled=True).reshape(-1, width)], 0
    chips = groups // 2
    chip = lax.axis_index("section") // 2
    by_chip = text_emb.reshape(chips, 2, piece, width)
    parts = [lax.dynamic_index_in_dim(by_chip, chip ^ k, 0, keepdims=False) for k in range(chips)]
    texts = parts[:1] + [exchange(parts[k], "section", 2 * k) for k in range(1, chips)]
    other = call(
        functools.partial(select_kernel, chips), "select", SHAPE((chips, piece, width), BF16),
        texts + early, LONG, specs=[VMEM] * chips + [ANY] * len(early))
    return texts + [exchange(other, "section", 1)], chips


def local(text_emb, covariate, labels, logit_scale, logit_bias):
    count = lax.axis_size("blk")
    rows, width = covariate.shape[1:]
    n_text = labels.shape[1]
    row = lax.broadcasted_iota(jnp.int32, (8, n_text), 0)
    params = jnp.where(row == 0, labels.astype(F32), jnp.where(row == 1, logit_scale[0], logit_bias[0]))
    covs, early = fetch_covs(covariate[0], count)
    texts, chips = fetch_texts(text_emb, early + [params])
    pile = call(pile_kernel, "pile", SHAPE((count * rows, width), BF16), covs, LONG)
    flops = 2 * count * rows * n_text * width
    coeff, own, *parts = call(
        functools.partial(coeff_kernel, count, chips), "coeff",
        [SHAPE((count * rows, n_text), BF16), SHAPE((rows, width), F32)] + [SHAPE((rows, width), BF16)] * (count - 1) + [SHAPE((rows, width), F32)] * two_cores(count),
        [params, pile] + texts, 2 * flops, limit=16 if count == 4 else 40,
        scratch=[pltpu.VMEM((n_text, width) if chips else (8, 128), BF16), pltpu.VMEM((count * rows, width), F32)])
    text_grad = call(text_kernel, "text_grad", SHAPE((n_text, width), F32), [coeff, pile], flops, limit=16)
    total = reduce_covs(own, parts, count)
    return text_grad[None], total[None]


def solution(mesh):
    return jax.shard_map(
        local,
        mesh=mesh,
        in_specs=(
            P(None, ("blk", "section"), None),
            P("section", "blk", None),
            P("section", "blk"),
            P(),
            P(),
        ),
        out_specs=(P("section", "blk", None), P("section", "blk", None)),
        check_vma=False,
    )
```

```python
import functools

import jax
import jax.numpy as jnp
from jax import lax
from jax.experimental import pallas as pl
from jax.experimental.pallas import tpu as pltpu
from jax.sharding import PartitionSpec as P

NT = (((1,), (1,)), ((), ()))
TN = (((0,), (0,)), ((), ()))
VMEM = pl.BlockSpec(memory_space=pltpu.VMEM)
ANY = pl.BlockSpec(memory_space=pl.ANY)
MIB = 2**20
BF16, F32 = jnp.bfloat16, jnp.float32
SHAPE = jax.ShapeDtypeStruct
LONG = 10**11


def is_power(count):
    return count & (count - 1) == 0


def exchange(value, axis, k):
    count = lax.axis_size(axis)
    return lax.ppermute(value, axis, [(i, i ^ k if is_power(count) else (i + k) % count) for i in range(count)])


def mixed(value, even, odd):
    blocks, groups = lax.axis_size("blk"), lax.axis_size("section")
    steps = [odd if s % 2 else even for s in range(groups)]
    pairs = [(b * groups + s, (b ^ steps[s]) * groups + s) for b in range(blocks) for s in range(groups) if steps[s]]
    return lax.ppermute(value, ("blk", "section"), pairs)


def source_block(me, k, count):
    return me ^ k if is_power(count) else lax.rem(me - k + count, jnp.int32(count))


def span(slot, rows):
    return pl.ds(pl.multiple_of(slot * rows, rows), rows)


def select_kernel(chips, *refs):
    section = lax.axis_index("section")
    chip, core = section // 2, section % 2
    out = refs[-1]
    out[0] = refs[0][chip, 1 - core]
    for k in range(1, chips):
        out[k] = refs[k][1 - core]


def sort_kernel(first_ref, second_ref, one_ref, two_ref):
    odd = lax.axis_index("section") % 2

    @pl.when(odd == 1)
    def _():
        one_ref[...] = first_ref[...]
        two_ref[...] = second_ref[...]

    @pl.when(odd == 0)
    def _():
        one_ref[...] = second_ref[...]
        two_ref[...] = first_ref[...]


def pile_kernel(*refs):
    *parts, out = refs
    rows = parts[0].shape[0]
    for k, part in enumerate(parts):
        out[k * rows:(k + 1) * rows, :] = part[...]


def coeff_kernel(count, chips, params_ref, covs_ref, *refs):
    texts, (coeff_ref, own_ref, *part_refs, panel) = refs[:chips + 1], refs[chips + 1:]
    rows = covs_ref.shape[0] // count
    if chips:
        section = lax.axis_index("section")
        chip, core = section // 2, section % 2
        piece = texts[0].shape[2]
        for k in range(chips):
            panel[span((chip ^ k) * 2 + core, piece), :] = texts[k][core] if k else texts[0][chip, core]
            panel[span((chip ^ k) * 2 + 1 - core, piece), :] = texts[chips][k]
        text_ref = panel
    else:
        text_ref = texts[0]
    labels, scale, bias = params_ref[0:1, :], params_ref[1:2, :], params_ref[2:3, :]
    logits = scale * lax.dot_general(covs_ref[...], text_ref[...], NT, preferred_element_type=F32) + bias
    me = lax.axis_index("blk")
    row = lax.broadcasted_iota(jnp.int32, (rows, 1), 0)
    ids = jnp.concatenate([source_block(me, k, count) * rows + row for k in range(count)], axis=0)
    positive = (labels == ids.astype(F32)).astype(F32)
    coeff = (scale * (jax.nn.sigmoid(logits) - positive)).astype(BF16)
    coeff_ref[...] = coeff
    step = min(256, text_ref.shape[1])
    for at in range(0, text_ref.shape[1], step):
        columns = slice(at, at + step)
        prod = jnp.dot(coeff, text_ref[:, columns], preferred_element_type=F32)
        blocks = [prod[k * rows:(k + 1) * rows, :] for k in range(count)]
        own_ref[:, columns] = blocks[0]
        if two_cores(count):
            first, second, third, far = part_refs
            first[:, columns] = blocks[2].astype(BF16)
            second[:, columns] = jnp.where(lax.axis_index("section") % 2 == 1, blocks[1], blocks[3]).astype(BF16)
            third[:, columns] = blocks[1].astype(BF16)
            far[:, columns] = blocks[3]
        else:
            for ref, block in zip(part_refs, blocks[1:]):
                ref[:, columns] = block.astype(BF16)


def add_kernel(part_ref, got_ref, out_ref):
    out_ref[...] = (part_ref[...] + got_ref[...].astype(F32)).astype(BF16)


def text_kernel(coeff_ref, covs_ref, out_ref):
    out_ref[...] = lax.dot_general(coeff_ref[...], covs_ref[...], TN, preferred_element_type=F32)


def call(kernel, name, out_shape, args, flops, scratch=(), limit=8, specs=None):
    many = isinstance(out_shape, list)
    return pl.pallas_call(
        kernel,
        out_shape=out_shape,
        in_specs=specs or [VMEM] * len(args),
        out_specs=[VMEM] * len(out_shape) if many else VMEM,
        scratch_shapes=list(scratch),
        compiler_params=pltpu.CompilerParams(vmem_limit_bytes=limit * MIB),
        cost_estimate=pl.CostEstimate(flops=flops, bytes_accessed=MIB, transcendentals=0),
        name=name,
    )(*args)


def two_cores(count):
    return count == 4 and lax.axis_size("section") % 2 == 0


def reduce_covs(own, parts, count):
    if not two_cores(count):
        got = [exchange(part, "blk", k if is_power(count) else -k) for k, part in enumerate(parts, 1)]
        return sum((part.astype(F32) for part in got), own)
    first, second, third, far = parts
    got = [mixed(first, 2, 1), mixed(second, 3, 1), mixed(third, 1, 0)]
    summed = call(add_kernel, "add", SHAPE(far.shape, BF16), [far, got[0]], 0)
    got.append(mixed(summed, 0, 3))
    odd = lax.axis_index("section") % 2 == 1
    return own + jnp.where(odd, 0, got[0].astype(F32)) + sum(part.astype(F32) for part in got[1:])


def fetch_covs(own, count):
    if count != 4:
        return [own] + [exchange(own, "blk", k) for k in range(1, count)], []
    got = [mixed(own, 2, 1), mixed(own, 1, 2)]
    one, two = call(sort_kernel, "sort", [SHAPE(own.shape, BF16)] * 2, got, 0)
    return [own, one, two, exchange(two, "blk", 1)], [two]


def fetch_texts(text_emb, early):
    groups, piece, width = text_emb.shape
    if not is_power(groups) or piece % 16:
        return [lax.all_to_all(text_emb, "section", 0, 0, tiled=True).reshape(-1, width)], 0
    chips = groups // 2
    chip = lax.axis_index("section") // 2
    by_chip = text_emb.reshape(chips, 2, piece, width)
    parts = [lax.dynamic_index_in_dim(by_chip, chip ^ k, 0, keepdims=False) for k in range(1, chips)]
    texts = [by_chip] + [exchange(part, "section", 2 * k) for k, part in enumerate(parts, 1)]
    other = call(
        functools.partial(select_kernel, chips), "select", SHAPE((chips, piece, width), BF16),
        texts + early, LONG, specs=[VMEM] * chips + [ANY] * len(early))
    return texts + [exchange(other, "section", 1)], chips


def local(text_emb, covariate, labels, logit_scale, logit_bias):
    count = lax.axis_size("blk")
    rows, width = covariate.shape[1:]
    n_text = labels.shape[1]
    row = lax.broadcasted_iota(jnp.int32, (8, n_text), 0)
    params = jnp.where(row == 0, labels.astype(F32), jnp.where(row == 1, logit_scale[0], logit_bias[0]))
    covs, early = fetch_covs(covariate[0], count)
    texts, chips = fetch_texts(text_emb, early + [params])
    pile = call(pile_kernel, "pile", SHAPE((count * rows, width), BF16), covs, LONG)
    flops = 2 * count * rows * n_text * width
    coeff, own, *parts = call(
        functools.partial(coeff_kernel, count, chips), "coeff",
        [SHAPE((count * rows, n_text), BF16), SHAPE((rows, width), F32)] + [SHAPE((rows, width), BF16)] * (count - 1) + [SHAPE((rows, width), F32)] * two_cores(count),
        [params, pile] + texts, 2 * flops, limit=16 if count == 4 else 40,
        scratch=[pltpu.VMEM((n_text, width) if chips else (16, 128), BF16)])
    text_grad = call(text_kernel, "text_grad", SHAPE((n_text, width), F32), [coeff, pile], flops, limit=16)
    total = reduce_covs(own, parts, count)
    return text_grad[None], total[None]


def solution(mesh):
    return jax.shard_map(
        local,
        mesh=mesh,
        in_specs=(
            P(None, ("blk", "section"), None),
            P("section", "blk", None),
            P("section", "blk"),
            P(),
            P(),
        ),
        out_specs=(P("section", "blk", None), P("section", "blk", None)),
        check_vma=False,
    )
```

```python
import functools

import jax
import jax.numpy as jnp
from jax import lax
from jax.experimental import pallas as pl
from jax.experimental.pallas import tpu as pltpu
from jax.sharding import PartitionSpec as P

NT = (((1,), (1,)), ((), ()))
TN = (((0,), (0,)), ((), ()))
VMEM = pl.BlockSpec(memory_space=pltpu.VMEM)
ANY = pl.BlockSpec(memory_space=pl.ANY)
MIB = 2**20
BF16, F32 = jnp.bfloat16, jnp.float32
SHAPE = jax.ShapeDtypeStruct
LONG = 10**11


def is_power(count):
    return count & (count - 1) == 0


def exchange(value, axis, k):
    count = lax.axis_size(axis)
    return lax.ppermute(value, axis, [(i, i ^ k if is_power(count) else (i + k) % count) for i in range(count)])


def mixed(value, even, odd):
    blocks, groups = lax.axis_size("blk"), lax.axis_size("section")
    steps = [odd if s % 2 else even for s in range(groups)]
    pairs = [(b * groups + s, (b ^ steps[s]) * groups + s) for b in range(blocks) for s in range(groups) if steps[s]]
    return lax.ppermute(value, ("blk", "section"), pairs)


def source_block(me, k, count):
    return me ^ k if is_power(count) else lax.rem(me - k + count, jnp.int32(count))


def span(slot, rows):
    return pl.ds(pl.multiple_of(slot * rows, rows), rows)


def select_kernel(chips, *refs):
    section = lax.axis_index("section")
    chip, core = section // 2, section % 2
    out = refs[-1]
    out[0] = refs[0][chip, 1 - core]
    for k in range(1, chips):
        out[k] = refs[k][1 - core]


def sort_kernel(first_ref, second_ref, one_ref, two_ref):
    odd = lax.axis_index("section") % 2

    @pl.when(odd == 1)
    def _():
        one_ref[...] = first_ref[...]
        two_ref[...] = second_ref[...]

    @pl.when(odd == 0)
    def _():
        one_ref[...] = second_ref[...]
        two_ref[...] = first_ref[...]


def pile_kernel(*refs):
    *parts, out = refs
    rows = parts[0].shape[0]
    for k, part in enumerate(parts):
        out[k * rows:(k + 1) * rows, :] = part[...]


def coeff_kernel(count, chips, params_ref, covs_ref, *refs):
    texts, (coeff_ref, own_ref, *part_refs, panel) = refs[:chips + 1], refs[chips + 1:]
    rows = covs_ref.shape[0] // count
    if chips:
        section = lax.axis_index("section")
        chip, core = section // 2, section % 2
        piece = texts[0].shape[2]
        for k in range(chips):
            panel[span((chip ^ k) * 2 + core, piece), :] = texts[k][core] if k else texts[0][chip, core]
            panel[span((chip ^ k) * 2 + 1 - core, piece), :] = texts[chips][k]
        text_ref = panel
    else:
        text_ref = texts[0]
    labels, scale, bias = params_ref[0:1, :], params_ref[1:2, :], params_ref[2:3, :]
    logits = scale * lax.dot_general(covs_ref[...], text_ref[...], NT, preferred_element_type=F32) + bias
    me = lax.axis_index("blk")
    row = lax.broadcasted_iota(jnp.int32, (rows, 1), 0)
    ids = jnp.concatenate([source_block(me, k, count) * rows + row for k in range(count)], axis=0)
    positive = (labels == ids.astype(F32)).astype(F32)
    coeff = (scale * (jax.nn.sigmoid(logits) - positive)).astype(BF16)
    coeff_ref[...] = coeff
    step = min(256, text_ref.shape[1])
    for at in range(0, text_ref.shape[1], step):
        columns = slice(at, at + step)
        prod = jnp.dot(coeff, text_ref[:, columns], preferred_element_type=F32)
        blocks = [prod[k * rows:(k + 1) * rows, :] for k in range(count)]
        own_ref[:, columns] = blocks[0]
        if two_cores(count):
            first, second, third, far = part_refs
            first[:, columns] = blocks[2].astype(BF16)
            second[:, columns] = jnp.where(lax.axis_index("section") % 2 == 1, blocks[1], blocks[3]).astype(BF16)
            third[:, columns] = blocks[1].astype(BF16)
            far[:, columns] = blocks[3]
        else:
            for ref, block in zip(part_refs, blocks[1:]):
                ref[:, columns] = block.astype(BF16)


def add_kernel(part_ref, got_ref, token_ref, out_ref):
    out_ref[...] = (part_ref[...] + got_ref[...].astype(F32)).astype(BF16)


def text_kernel(coeff_ref, covs_ref, out_ref, token_ref):
    token_ref[...] = jnp.zeros_like(token_ref)
    out_ref[...] = lax.dot_general(coeff_ref[...], covs_ref[...], TN, preferred_element_type=F32)


def call(kernel, name, out_shape, args, flops, scratch=(), limit=8, specs=None):
    many = isinstance(out_shape, list)
    return pl.pallas_call(
        kernel,
        out_shape=out_shape,
        in_specs=specs or [VMEM] * len(args),
        out_specs=[VMEM] * len(out_shape) if many else VMEM,
        scratch_shapes=list(scratch),
        compiler_params=pltpu.CompilerParams(vmem_limit_bytes=limit * MIB),
        cost_estimate=pl.CostEstimate(flops=flops, bytes_accessed=MIB, transcendentals=0),
        name=name,
    )(*args)


def two_cores(count):
    return count == 4 and lax.axis_size("section") % 2 == 0


def reduce_covs(own, parts, count, token):
    if not two_cores(count):
        got = [exchange(part, "blk", k if is_power(count) else -k) for k, part in enumerate(parts, 1)]
        return sum((part.astype(F32) for part in got), own)
    first, second, third, far = parts
    got = [mixed(first, 2, 1), mixed(second, 3, 1), mixed(third, 1, 0)]
    summed = call(add_kernel, "add", SHAPE(far.shape, BF16), [far, got[0], token], 0)
    got.append(mixed(summed, 0, 3))
    odd = lax.axis_index("section") % 2 == 1
    return own + jnp.where(odd, 0, got[0].astype(F32)) + sum(part.astype(F32) for part in got[1:])


def fetch_covs(own, count):
    if count != 4:
        return [own] + [exchange(own, "blk", k) for k in range(1, count)], []
    got = [mixed(own, 2, 1), mixed(own, 1, 2)]
    one, two = call(sort_kernel, "sort", [SHAPE(own.shape, BF16)] * 2, got, 0)
    return [own, one, two, exchange(two, "blk", 1)], [two]


def fetch_texts(text_emb, early):
    groups, piece, width = text_emb.shape
    if not is_power(groups) or piece % 16:
        return [lax.all_to_all(text_emb, "section", 0, 0, tiled=True).reshape(-1, width)], 0
    chips = groups // 2
    chip = lax.axis_index("section") // 2
    by_chip = text_emb.reshape(chips, 2, piece, width)
    parts = [lax.dynamic_index_in_dim(by_chip, chip ^ k, 0, keepdims=False) for k in range(1, chips)]
    texts = [by_chip] + [exchange(part, "section", 2 * k) for k, part in enumerate(parts, 1)]
    other = call(
        functools.partial(select_kernel, chips), "select", SHAPE((chips, piece, width), BF16),
        texts + early, LONG, specs=[VMEM] * chips + [ANY] * len(early))
    return texts + [exchange(other, "section", 1)], chips


def local(text_emb, covariate, labels, logit_scale, logit_bias):
    count = lax.axis_size("blk")
    rows, width = covariate.shape[1:]
    n_text = labels.shape[1]
    row = lax.broadcasted_iota(jnp.int32, (8, n_text), 0)
    params = jnp.where(row == 0, labels.astype(F32), jnp.where(row == 1, logit_scale[0], logit_bias[0]))
    covs, early = fetch_covs(covariate[0], count)
    texts, chips = fetch_texts(text_emb, early + [params])
    pile = call(pile_kernel, "pile", SHAPE((count * rows, width), BF16), covs, LONG)
    flops = 2 * count * rows * n_text * width
    coeff, own, *parts = call(
        functools.partial(coeff_kernel, count, chips), "coeff",
        [SHAPE((count * rows, n_text), BF16), SHAPE((rows, width), F32)] + [SHAPE((rows, width), BF16)] * (count - 1) + [SHAPE((rows, width), F32)] * two_cores(count),
        [params, pile] + texts, 2 * flops, limit=16 if count == 4 else 40,
        scratch=[pltpu.VMEM((n_text, width) if chips else (16, 128), BF16)])
    text_grad, token = call(text_kernel, "text_grad", [SHAPE((n_text, width), F32), SHAPE((8, 128), F32)], [coeff, pile], flops, limit=16)
    total = reduce_covs(own, parts, count, token)
    return text_grad[None], total[None]


def solution(mesh):
    return jax.shard_map(
        local,
        mesh=mesh,
        in_specs=(
            P(None, ("blk", "section"), None),
            P("section", "blk", None),
            P("section", "blk"),
            P(),
            P(),
        ),
        out_specs=(P("section", "blk", None), P("section", "blk", None)),
        check_vma=False,
    )
```

```python
import functools

import jax
import jax.numpy as jnp
from jax import lax
from jax.experimental import pallas as pl
from jax.experimental.pallas import tpu as pltpu
from jax.sharding import PartitionSpec as P

NT = (((1,), (1,)), ((), ()))
TN = (((0,), (0,)), ((), ()))
VMEM = pl.BlockSpec(memory_space=pltpu.VMEM)
ANY = pl.BlockSpec(memory_space=pl.ANY)
MIB = 2**20
BF16, F32 = jnp.bfloat16, jnp.float32
SHAPE = jax.ShapeDtypeStruct
LONG = 10**11


def is_power(count):
    return count & (count - 1) == 0


def exchange(value, axis, k):
    count = lax.axis_size(axis)
    return lax.ppermute(value, axis, [(i, i ^ k if is_power(count) else (i + k) % count) for i in range(count)])


def mixed(value, even, odd):
    blocks, groups = lax.axis_size("blk"), lax.axis_size("section")
    steps = [odd if s % 2 else even for s in range(groups)]
    pairs = [(b * groups + s, (b ^ steps[s]) * groups + s) for b in range(blocks) for s in range(groups) if steps[s]]
    return lax.ppermute(value, ("blk", "section"), pairs)


def source_block(me, k, count):
    return me ^ k if is_power(count) else lax.rem(me - k + count, jnp.int32(count))


def span(slot, rows):
    return pl.ds(pl.multiple_of(slot * rows, rows), rows)


def select_kernel(chips, *refs):
    section = lax.axis_index("section")
    chip, core = section // 2, section % 2
    out = refs[-1]
    out[0] = refs[0][chip, 1 - core]
    for k in range(1, chips):
        out[k] = refs[k][1 - core]


def sort_kernel(first_ref, second_ref, one_ref, two_ref):
    odd = lax.axis_index("section") % 2

    @pl.when(odd == 1)
    def _():
        one_ref[...] = first_ref[...]
        two_ref[...] = second_ref[...]

    @pl.when(odd == 0)
    def _():
        one_ref[...] = second_ref[...]
        two_ref[...] = first_ref[...]


def pile_kernel(*refs):
    *parts, out = refs
    rows = parts[0].shape[0]
    for k, part in enumerate(parts):
        out[k * rows:(k + 1) * rows, :] = part[...]


def coeff_kernel(count, chips, params_ref, covs_ref, *refs):
    texts, (coeff_ref, own_ref, *part_refs, panel) = refs[:chips + 1], refs[chips + 1:]
    rows = covs_ref.shape[0] // count
    if chips:
        section = lax.axis_index("section")
        chip, core = section // 2, section % 2
        piece = texts[0].shape[2]
        for k in range(chips):
            panel[span((chip ^ k) * 2 + core, piece), :] = texts[k][core] if k else texts[0][chip, core]
            panel[span((chip ^ k) * 2 + 1 - core, piece), :] = texts[chips][k]
        text_ref = panel
    else:
        text_ref = texts[0]
    labels, scale, bias = params_ref[0:1, :], params_ref[1:2, :], params_ref[2:3, :]
    logits = scale * lax.dot_general(covs_ref[...], text_ref[...], NT, preferred_element_type=F32) + bias
    me = lax.axis_index("blk")
    row = lax.broadcasted_iota(jnp.int32, (rows, 1), 0)
    ids = jnp.concatenate([source_block(me, k, count) * rows + row for k in range(count)], axis=0)
    positive = (labels == ids.astype(F32)).astype(F32)
    coeff = (scale * (jax.nn.sigmoid(logits) - positive)).astype(BF16)
    coeff_ref[...] = coeff
    step = min(256, text_ref.shape[1])
    for at in range(0, text_ref.shape[1], step):
        columns = slice(at, at + step)
        prod = jnp.dot(coeff, text_ref[:, columns], preferred_element_type=F32)
        blocks = [prod[k * rows:(k + 1) * rows, :] for k in range(count)]
        own_ref[:, columns] = blocks[0]
        if two_cores(count):
            first, second, third, far = part_refs
            first[:, columns] = blocks[2].astype(BF16)
            second[:, columns] = jnp.where(lax.axis_index("section") % 2 == 1, blocks[1], blocks[3]).astype(BF16)
            third[:, columns] = blocks[1].astype(BF16)
            far[:, columns] = blocks[3]
        else:
            for ref, block in zip(part_refs, blocks[1:]):
                ref[:, columns] = block.astype(BF16)


def add_kernel(part_ref, got_ref, out_ref):
    out_ref[...] = (part_ref[...] + got_ref[...].astype(F32)).astype(BF16)


def text_kernel(coeff_ref, covs_ref, out_ref):
    out_ref[...] = lax.dot_general(coeff_ref[...], covs_ref[...], TN, preferred_element_type=F32)


def call(kernel, name, out_shape, args, flops, scratch=(), limit=8, specs=None):
    many = isinstance(out_shape, list)
    return pl.pallas_call(
        kernel,
        out_shape=out_shape,
        in_specs=specs or [VMEM] * len(args),
        out_specs=[VMEM] * len(out_shape) if many else VMEM,
        scratch_shapes=list(scratch),
        compiler_params=pltpu.CompilerParams(vmem_limit_bytes=limit * MIB),
        cost_estimate=pl.CostEstimate(flops=flops, bytes_accessed=MIB, transcendentals=0),
        name=name,
    )(*args)


def two_cores(count):
    return count == 4 and lax.axis_size("section") % 2 == 0


def reduce_covs(own, parts, count):
    if not two_cores(count):
        got = [exchange(part, "blk", k if is_power(count) else -k) for k, part in enumerate(parts, 1)]
        return sum((part.astype(F32) for part in got), own)
    first, second, third, far = parts
    near = mixed(third, 1, 0)
    got = [mixed(first, 2, 1), mixed(second, 3, 1), near]
    summed = call(add_kernel, "add", SHAPE(far.shape, BF16), [far, got[0]], 0)
    got.append(mixed(summed, 0, 3))
    odd = lax.axis_index("section") % 2 == 1
    return own + jnp.where(odd, 0, got[0].astype(F32)) + sum(part.astype(F32) for part in got[1:])


def fetch_covs(own, count):
    if count != 4:
        return [own] + [exchange(own, "blk", k) for k in range(1, count)], []
    got = [mixed(own, 2, 1), mixed(own, 1, 2)]
    one, two = call(sort_kernel, "sort", [SHAPE(own.shape, BF16)] * 2, got, 0)
    return [own, one, two, exchange(two, "blk", 1)], [two]


def fetch_texts(text_emb, early):
    groups, piece, width = text_emb.shape
    if not is_power(groups) or piece % 16:
        return [lax.all_to_all(text_emb, "section", 0, 0, tiled=True).reshape(-1, width)], 0
    chips = groups // 2
    chip = lax.axis_index("section") // 2
    by_chip = text_emb.reshape(chips, 2, piece, width)
    parts = [lax.dynamic_index_in_dim(by_chip, chip ^ k, 0, keepdims=False) for k in range(1, chips)]
    texts = [by_chip] + [exchange(part, "section", 2 * k) for k, part in enumerate(parts, 1)]
    other = call(
        functools.partial(select_kernel, chips), "select", SHAPE((chips, piece, width), BF16),
        texts + early, LONG, specs=[VMEM] * chips + [ANY] * len(early))
    return texts + [exchange(other, "section", 1)], chips


def local(text_emb, covariate, labels, logit_scale, logit_bias):
    count = lax.axis_size("blk")
    rows, width = covariate.shape[1:]
    n_text = labels.shape[1]
    row = lax.broadcasted_iota(jnp.int32, (8, n_text), 0)
    params = jnp.where(row == 0, labels.astype(F32), jnp.where(row == 1, logit_scale[0], logit_bias[0]))
    covs, early = fetch_covs(covariate[0], count)
    texts, chips = fetch_texts(text_emb, early + [params])
    pile = call(pile_kernel, "pile", SHAPE((count * rows, width), BF16), covs, LONG)
    flops = 2 * count * rows * n_text * width
    coeff, own, *parts = call(
        functools.partial(coeff_kernel, count, chips), "coeff",
        [SHAPE((count * rows, n_text), BF16), SHAPE((rows, width), F32)] + [SHAPE((rows, width), BF16)] * (count - 1) + [SHAPE((rows, width), F32)] * two_cores(count),
        [params, pile] + texts, 2 * flops, limit=16 if count == 4 else 40,
        scratch=[pltpu.VMEM((n_text, width) if chips else (16, 128), BF16)])
    text_grad = call(text_kernel, "text_grad", SHAPE((n_text, width), F32), [coeff, pile], flops, limit=16)
    total = reduce_covs(own, parts, count)
    return text_grad[None], total[None]


def solution(mesh):
    return jax.shard_map(
        local,
        mesh=mesh,
        in_specs=(
            P(None, ("blk", "section"), None),
            P("section", "blk", None),
            P("section", "blk"),
            P(),
            P(),
        ),
        out_specs=(P("section", "blk", None), P("section", "blk", None)),
        check_vma=False,
    )
```

```python
import functools

import jax
import jax.numpy as jnp
from jax import lax
from jax.experimental import pallas as pl
from jax.experimental.pallas import tpu as pltpu
from jax.sharding import PartitionSpec as P

NT = (((1,), (1,)), ((), ()))
TN = (((0,), (0,)), ((), ()))
VMEM = pl.BlockSpec(memory_space=pltpu.VMEM)
ANY = pl.BlockSpec(memory_space=pl.ANY)
MIB = 2**20
BF16, F32 = jnp.bfloat16, jnp.float32
SHAPE = jax.ShapeDtypeStruct
LONG = 10**11


def is_power(count):
    return count & (count - 1) == 0


def exchange(value, axis, k):
    count = lax.axis_size(axis)
    return lax.ppermute(value, axis, [(i, i ^ k if is_power(count) else (i + k) % count) for i in range(count)])


def mixed(value, even, odd):
    blocks, groups = lax.axis_size("blk"), lax.axis_size("section")
    steps = [odd if s % 2 else even for s in range(groups)]
    pairs = [(b * groups + s, (b ^ steps[s]) * groups + s) for b in range(blocks) for s in range(groups) if steps[s]]
    return lax.ppermute(value, ("blk", "section"), pairs)


def source_block(me, k, count):
    return me ^ k if is_power(count) else lax.rem(me - k + count, jnp.int32(count))


def span(slot, rows):
    return pl.ds(pl.multiple_of(slot * rows, rows), rows)


def select_kernel(chips, *refs):
    section = lax.axis_index("section")
    chip, core = section // 2, section % 2
    out = refs[-1]
    out[0] = refs[0][chip, 1 - core]
    for k in range(1, chips):
        out[k] = refs[k][1 - core]


def sort_kernel(first_ref, second_ref, one_ref, two_ref):
    odd = lax.axis_index("section") % 2

    @pl.when(odd == 1)
    def _():
        one_ref[...] = first_ref[...]
        two_ref[...] = second_ref[...]

    @pl.when(odd == 0)
    def _():
        one_ref[...] = second_ref[...]
        two_ref[...] = first_ref[...]


def pile_kernel(*refs):
    *parts, out = refs
    rows = parts[0].shape[0]
    for k, part in enumerate(parts):
        out[k * rows:(k + 1) * rows, :] = part[...]


def coeff_kernel(count, chips, params_ref, covs_ref, *refs):
    texts, (coeff_ref, own_ref, *part_refs, panel) = refs[:chips + 1], refs[chips + 1:]
    rows = covs_ref.shape[0] // count
    if chips:
        section = lax.axis_index("section")
        chip, core = section // 2, section % 2
        piece = texts[0].shape[2]
        for k in range(chips):
            panel[span((chip ^ k) * 2 + core, piece), :] = texts[k][core] if k else texts[0][chip, core]
            panel[span((chip ^ k) * 2 + 1 - core, piece), :] = texts[chips][k]
        text_ref = panel
    else:
        text_ref = texts[0]
    labels, scale, bias = params_ref[0:1, :], params_ref[1:2, :], params_ref[2:3, :]
    logits = scale * lax.dot_general(covs_ref[...], text_ref[...], NT, preferred_element_type=F32) + bias
    me = lax.axis_index("blk")
    row = lax.broadcasted_iota(jnp.int32, (rows, 1), 0)
    ids = jnp.concatenate([source_block(me, k, count) * rows + row for k in range(count)], axis=0)
    positive = (labels == ids.astype(F32)).astype(F32)
    coeff = (scale * (jax.nn.sigmoid(logits) - positive)).astype(BF16)
    coeff_ref[...] = coeff
    step = min(256, text_ref.shape[1])
    for at in range(0, text_ref.shape[1], step):
        columns = slice(at, at + step)
        prod = jnp.dot(coeff, text_ref[:, columns], preferred_element_type=F32)
        blocks = [prod[k * rows:(k + 1) * rows, :] for k in range(count)]
        own_ref[:, columns] = blocks[0]
        if two_cores(count):
            first, second, third, far = part_refs
            first[:, columns] = blocks[2].astype(BF16)
            second[:, columns] = jnp.where(lax.axis_index("section") % 2 == 1, blocks[1], blocks[3]).astype(BF16)
            third[:, columns] = blocks[1].astype(BF16)
            far[:, columns] = blocks[3]
        else:
            for ref, block in zip(part_refs, blocks[1:]):
                ref[:, columns] = block.astype(BF16)


def add_kernel(part_ref, got_ref, out_ref):
    out_ref[...] = (part_ref[...] + got_ref[...].astype(F32)).astype(BF16)


def text_kernel(coeff_ref, covs_ref, out_ref):
    out_ref[...] = lax.dot_general(coeff_ref[...], covs_ref[...], TN, preferred_element_type=F32)


def call(kernel, name, out_shape, args, flops, scratch=(), limit=8, specs=None):
    many = isinstance(out_shape, list)
    return pl.pallas_call(
        kernel,
        out_shape=out_shape,
        in_specs=specs or [VMEM] * len(args),
        out_specs=[VMEM] * len(out_shape) if many else VMEM,
        scratch_shapes=list(scratch),
        compiler_params=pltpu.CompilerParams(vmem_limit_bytes=limit * MIB),
        cost_estimate=pl.CostEstimate(flops=flops, bytes_accessed=MIB, transcendentals=0),
        name=name,
    )(*args)


def two_cores(count):
    return count == 4 and lax.axis_size("section") % 2 == 0


def reduce_covs(own, parts, count):
    if not two_cores(count):
        got = [exchange(part, "blk", k if is_power(count) else -k) for k, part in enumerate(parts, 1)]
        return sum((part.astype(F32) for part in got), own)
    first, second, third, far = parts
    straight = mixed(second, 3, 1)
    got = [mixed(first, 2, 1), straight, mixed(third, 1, 0)]
    summed = call(add_kernel, "add", SHAPE(far.shape, BF16), [far, got[0]], 0)
    got.append(mixed(summed, 0, 3))
    odd = lax.axis_index("section") % 2 == 1
    return own + jnp.where(odd, 0, got[0].astype(F32)) + sum(part.astype(F32) for part in got[1:])


def fetch_covs(own, count):
    if count != 4:
        return [own] + [exchange(own, "blk", k) for k in range(1, count)], []
    got = [mixed(own, 2, 1), mixed(own, 1, 2)]
    one, two = call(sort_kernel, "sort", [SHAPE(own.shape, BF16)] * 2, got, 0)
    return [own, one, two, exchange(two, "blk", 1)], [two]


def fetch_texts(text_emb, early):
    groups, piece, width = text_emb.shape
    if not is_power(groups) or piece % 16:
        return [lax.all_to_all(text_emb, "section", 0, 0, tiled=True).reshape(-1, width)], 0
    chips = groups // 2
    chip = lax.axis_index("section") // 2
    by_chip = text_emb.reshape(chips, 2, piece, width)
    parts = [lax.dynamic_index_in_dim(by_chip, chip ^ k, 0, keepdims=False) for k in range(1, chips)]
    texts = [by_chip] + [exchange(part, "section", 2 * k) for k, part in enumerate(parts, 1)]
    other = call(
        functools.partial(select_kernel, chips), "select", SHAPE((chips, piece, width), BF16),
        texts + early, LONG, specs=[VMEM] * chips + [ANY] * len(early))
    return texts + [exchange(other, "section", 1)], chips


def local(text_emb, covariate, labels, logit_scale, logit_bias):
    count = lax.axis_size("blk")
    rows, width = covariate.shape[1:]
    n_text = labels.shape[1]
    row = lax.broadcasted_iota(jnp.int32, (8, n_text), 0)
    params = jnp.where(row == 0, labels.astype(F32), jnp.where(row == 1, logit_scale[0], logit_bias[0]))
    covs, early = fetch_covs(covariate[0], count)
    texts, chips = fetch_texts(text_emb, early + [params])
    pile = call(pile_kernel, "pile", SHAPE((count * rows, width), BF16), covs, LONG)
    flops = 2 * count * rows * n_text * width
    coeff, own, *parts = call(
        functools.partial(coeff_kernel, count, chips), "coeff",
        [SHAPE((count * rows, n_text), BF16), SHAPE((rows, width), F32)] + [SHAPE((rows, width), BF16)] * (count - 1) + [SHAPE((rows, width), F32)] * two_cores(count),
        [params, pile] + texts, 2 * flops, limit=16 if count == 4 else 40,
        scratch=[pltpu.VMEM((n_text, width) if chips else (16, 128), BF16)])
    text_grad = call(text_kernel, "text_grad", SHAPE((n_text, width), F32), [coeff, pile], flops, limit=16)
    total = reduce_covs(own, parts, count)
    return text_grad[None], total[None]


def solution(mesh):
    return jax.shard_map(
        local,
        mesh=mesh,
        in_specs=(
            P(None, ("blk", "section"), None),
            P("section", "blk", None),
            P("section", "blk"),
            P(),
            P(),
        ),
        out_specs=(P("section", "blk", None), P("section", "blk", None)),
        check_vma=False,
    )
```
